256 devices in a mesh: outer: 16 (over x, y), inner: 16 (over z, core).
Axes of the slice: x: 4, y: 4, z: 8, core: 2. Of those that a mesh axis runs over, the one named last changes fastest.
Arguments:
- queries: bfloat16 [65536, 1024], P(('outer', 'inner')), may hold values from -6 to 6
- out_grad: bfloat16 [65536, 1024], P(('outer', 'inner')), may hold values from -1.5 to 1.5
- logsumexp: float32 [8, 65536], P(None, ('outer', 'inner')), may hold values from 4 to 8
- row_delta: float32 [8, 65536], P(None, ('outer', 'inner')), may hold values from -6 to 6
- doc_offset: int32 [65536], P(('outer', 'inner')), may hold values from 0 to 3071, as said below
- key_states: bfloat16 [65536, 128], P(('outer', 'inner')), may hold values from -6 to 6
- value_states: bfloat16 [65536, 128], P(('outer', 'inner')), may hold values from -6 to 6
Outputs:
- query_grad: bfloat16 [65536, 1024], P(('outer', 'inner'))
- key_grad: bfloat16 [65536, 128], P(('outer', 'inner'))
- value_grad: bfloat16 [65536, 128], P(('outer', 'inner'))
The draws below stay inside these ranges and needn't reach their ends.
Inputs may be any that keep to these rules, and one draw needn't show every extreme that they name: `doc_offset`: documents are contiguous runs of tokens whose entries count 0, 1, 2, ...; a new document starts wherever the entry is 0. Each document holds at most 3072 tokens and one holds exactly 3072.
All inputs are finite; a program needn't handle non-finite values.
Results may differ from the reference program's by a relative error of at most 0.0054.
Values may be sent and summed in bfloat16 or wider, within the bound.
A program may use at most 128 MiB of HBM per device.

```python
import math
import jax
import jax.numpy as jnp
from jax import lax

H = 8
DH = 128
TOK_DEV = 256
REACH = 12
MAXDOC = 3072
TOKENS = 65536


def draw_doc_offset(key, part):
    key = jax.random.fold_in(key, 7)
    first_key, second_key = jax.random.split(key)
    lengths = jax.random.randint(first_key, (TOKENS,), 1, MAXDOC + 1, dtype=jnp.int32)
    chosen = jax.random.randint(second_key, (), 0, 4, dtype=jnp.int32)
    counter = jnp.arange(TOKENS, dtype=jnp.int32)
    lengths = jnp.where(counter == chosen, jnp.int32(MAXDOC), lengths)
    ends = jnp.cumsum(lengths).astype(jnp.int32)
    starts = ends - lengths
    which = jnp.searchsorted(ends, counter, side='right').astype(jnp.int32)
    return (counter - starts[which]).astype(jnp.int32)


def level_of(rng, dims, shards, least, largest):
    loudness, own = 1.0, jax.random.fold_in(rng, 6)
    for axis_at, blocks in shards:
        steps = jnp.exp(jax.random.uniform(jax.random.fold_in(own, axis_at), (blocks,), jnp.float32, least / len(shards), largest / len(shards)))
        loudness = loudness * jnp.repeat(steps, dims[axis_at] // blocks).reshape([-1 if axis == axis_at else 1 for axis in range(len(dims))])
    return loudness


def gaussian(stream_key, shape, deviation, limit, cuts=(), kind=jnp.bfloat16):
    array = deviation * jax.random.normal(stream_key, shape, jnp.float32)
    if cuts:
        array = array * level_of(stream_key, shape, cuts, -0.22, 0.18)
    return jnp.clip(array, -limit, limit).astype(kind)


def setup_inputs(seed: int = 0) -> dict:
    splits = jax.random.split(jax.random.key(seed), 8)
    queries = gaussian(splits[0], (TOKENS, H * DH), 1.0, 6.0, ((0, 256),))
    out_grad = gaussian(splits[1], (TOKENS, H * DH), 0.25, 1.5, ((0, 256),))
    logsumexp = jnp.clip(4.0 + 4.0 * jax.random.uniform(splits[2], (H, TOKENS), jnp.float32) ** level_of(splits[2], (H, TOKENS), ((1, 256),), -0.2, 0.2), 4.0, 8.0)
    row_delta = gaussian(splits[3], (H, TOKENS), 1.0, 6.0, ((1, 256),), jnp.float32)
    doc_offset = draw_doc_offset(jax.random.fold_in(splits[7], 71), 0)
    key_states = gaussian(splits[5], (TOKENS, DH), 1.0, 6.0, ((0, 256),))
    value_states = gaussian(splits[6], (TOKENS, DH), 1.0, 6.0, ((0, 256),))
    return {"queries": queries, "out_grad": out_grad, "logsumexp": logsumexp, "row_delta": row_delta, "doc_offset": doc_offset, "key_states": key_states, "value_states": value_states}


def pair_grads(queries, out_grad, logsumexp, row_delta, row_first, query_pos, key_states, value_states, key_pos):
    head_size = key_states.shape[1]
    head_count = logsumexp.shape[0]
    inv_root = 1.0 / math.sqrt(head_size)
    allowed = (key_pos[None, :] <= query_pos[:, None]) & (key_pos[None, :] >= row_first[:, None])
    zero_keys = jnp.zeros(key_states.shape, jnp.float32)
    zero_rows = jnp.zeros(queries.shape, jnp.float32)

    def one_head(running, head_idx):
        grad_q, grad_k, grad_v = running
        query_h = lax.dynamic_slice_in_dim(queries, head_idx * head_size, head_size, 1)
        dout_h = lax.dynamic_slice_in_dim(out_grad, head_idx * head_size, head_size, 1)
        norm_h = lax.dynamic_index_in_dim(logsumexp, head_idx, 0, keepdims=False)
        delta_h = lax.dynamic_index_in_dim(row_delta, head_idx, 0, keepdims=False)
        scores = jnp.dot(query_h, key_states.T, preferred_element_type=jnp.float32) * inv_root
        prob = jnp.where(allowed, jnp.exp(scores - norm_h[:, None]), jnp.zeros_like(scores))
        prob_b = prob.astype(jnp.bfloat16)
        dprob = jnp.dot(dout_h, value_states.T, preferred_element_type=jnp.float32)
        dscore = (prob * (dprob - delta_h[:, None])).astype(jnp.bfloat16)
        piece = jnp.dot(dscore, key_states, preferred_element_type=jnp.float32) * inv_root
        grad_q = lax.dynamic_update_slice_in_dim(grad_q, piece, head_idx * head_size, 1)
        grad_k = grad_k + jnp.dot(dscore.T, query_h, preferred_element_type=jnp.float32) * inv_root
        grad_v = grad_v + jnp.dot(prob_b.T, dout_h, preferred_element_type=jnp.float32)
        return ((grad_q, grad_k, grad_v), None)
    results, _ = lax.scan(one_head, (zero_rows, zero_keys, zero_keys), jnp.arange(head_count, dtype=jnp.int32))
    return results

def reference(queries, out_grad, logsumexp, row_delta, doc_offset, key_states, value_states):
    all_rows = queries.shape[0]
    margin = REACH * TOK_DEV
    window = margin + TOK_DEV
    blank = jnp.zeros((margin, key_states.shape[1]), key_states.dtype)
    keys_pad = jnp.concatenate([blank, key_states], axis=0)
    values_pad = jnp.concatenate([blank, value_states], axis=0)
    positions = jnp.arange(all_rows, dtype=jnp.int32)
    firsts = positions - doc_offset.astype(jnp.int32)
    padded_pos = jnp.arange(all_rows + margin, dtype=jnp.int32) - margin

    def one_block(running, block_idx):
        grad_k, grad_v = running
        row_start = (block_idx * TOK_DEV).astype(jnp.int32)
        query_b = lax.dynamic_slice_in_dim(queries, row_start, TOK_DEV, 0)
        dout_b = lax.dynamic_slice_in_dim(out_grad, row_start, TOK_DEV, 0)
        norm_b = lax.dynamic_slice_in_dim(logsumexp, row_start, TOK_DEV, 1)
        delta_b = lax.dynamic_slice_in_dim(row_delta, row_start, TOK_DEV, 1)
        first_b = lax.dynamic_slice_in_dim(firsts, row_start, TOK_DEV, 0)
        pos_b = lax.dynamic_slice_in_dim(positions, row_start, TOK_DEV, 0)
        key_b = lax.dynamic_slice_in_dim(keys_pad, row_start, window, 0)
        value_b = lax.dynamic_slice_in_dim(values_pad, row_start, window, 0)
        kpos_b = lax.dynamic_slice_in_dim(padded_pos, row_start, window, 0)
        part_q, part_k, part_v = pair_grads(query_b, dout_b, norm_b, delta_b, first_b, pos_b, key_b, value_b, kpos_b)
        grad_k = lax.dynamic_update_slice_in_dim(grad_k, lax.dynamic_slice_in_dim(grad_k, row_start, window, 0) + part_k, row_start, 0)
        grad_v = lax.dynamic_update_slice_in_dim(grad_v, lax.dynamic_slice_in_dim(grad_v, row_start, window, 0) + part_v, row_start, 0)
        return ((grad_k, grad_v), part_q.astype(jnp.bfloat16))
    start_grads = jnp.zeros((all_rows + margin, key_states.shape[1]), jnp.float32)
    (grad_k, grad_v), grad_q = lax.scan(one_block, (start_grads, start_grads), jnp.arange(all_rows // TOK_DEV, dtype=jnp.int32))
    query_grad = grad_q.reshape(all_rows, queries.shape[1])
    return (query_grad, grad_k[margin:].astype(jnp.bfloat16), grad_v[margin:].astype(jnp.bfloat16))
```

```python
import math

import jax
import jax.numpy as jnp
from jax import lax
from jax.experimental import pallas as pl
from jax.experimental.pallas import tpu as pltpu
from jax.sharding import PartitionSpec as P

MESH = pl.DeviceIdType.MESH
F32 = jnp.float32
BF16 = jnp.bfloat16
HEADS = 8
DH = 128
TOK = 256
UNITS = 13
SCALE = 1.0 / math.sqrt(DH)
LOG2E = math.log2(math.e)


def dot_nt(a, b):
    return lax.dot_general(a, b, (((1,), (1,)), ((), ())), preferred_element_type=F32)


def dot_nn(a, b):
    return jnp.dot(a, b, preferred_element_type=F32)


def kernel(
    q_hbm, do_hbm, lse_hbm, del_hbm, off_hbm, k_hbm, v_hbm,
    dq_out, dk_out, dv_out,
    q_buf, do_buf, lse_buf, del_buf, off_buf, kv, acc, dqt, dq_in, stage, came_in,
    dq_st, dkv_st,
    load_sem, ex_send, ex_recv, kv_send, kv_recv, g_send, g_recv, dq_sem, out_sem,
):
    outer, inner = lax.axis_size("outer"), lax.axis_size("inner")
    total = outer * inner
    me = lax.axis_index("outer") * inner + lax.axis_index("inner")
    core = lax.rem(me, 2)
    greet = jnp.where(lax.axis_index("inner") < 8, 1, 0)

    def at(chips):
        there = lax.rem(me + 2 * chips + total, total)
        return (lax.div(there, inner), lax.rem(there, inner))

    sib_index = me + 1 - 2 * core
    sibling = (lax.div(sib_index, inner), lax.rem(sib_index, inner))

    loads = [
        pltpu.make_async_copy(src, dst, load_sem.at[n])
        for n, (src, dst) in enumerate((
            (k_hbm, kv.at[0, 0]), (v_hbm, kv.at[0, 1]),
            (q_hbm, q_buf.at[0]), (do_hbm, do_buf.at[0]),
            (lse_hbm, lse_buf.at[0]), (del_hbm, del_buf.at[0]), (off_hbm, off_buf.at[0]),
        ))
    ]
    for load in loads:
        load.start()

    barrier = pltpu.get_barrier_semaphore()
    partners = [sibling] + [at(chips) for chips in (1, -1, 6, -6)]
    for partner in partners:
        pl.semaphore_signal(barrier, inc=1, device_id=partner, device_id_type=MESH)

    def remote(src, dst, send, recv, where):
        return pltpu.make_async_remote_copy(
            src_ref=src, dst_ref=dst, send_sem=send, recv_sem=recv, device_id=where, device_id_type=MESH
        )

    exchange = [
        remote(src, dst, ex_send.at[n], ex_recv.at[n], sibling)
        for n, (src, dst) in enumerate((
            (q_hbm, q_buf.at[1]), (do_hbm, do_buf.at[1]),
            (lse_hbm, lse_buf.at[1]), (del_hbm, del_buf.at[1]), (off_hbm, off_buf.at[1]),
        ))
    ]
    kv_from = {1: (0, 1), 2: (1, 1), 3: (2, 1), 4: (3, 1), 6: (0, 6), 5: (6, -1)}
    kv_copy = {
        j: remote(kv.at[src], kv.at[j], kv_send.at[j], kv_recv.at[j], at(chips))
        for j, (src, chips) in kv_from.items()
    }
    g_to = {j: (came_in.at[j], -1) for j in (3, 2, 1)} | {j: (came_in.at[j], 1) for j in (4, 5)} | {6: (came_in.at[6], -6)}
    g_copy = {
        j: remote(stage.at[j], dst, g_send.at[j], g_recv.at[j], at(chips)) for j, (dst, chips) in g_to.items()
    }
    dq_copy = remote(dqt.at[1], dq_in, dq_sem.at[0], dq_sem.at[1], sibling)

    acc[...] = jnp.zeros_like(acc)
    dqt[...] = jnp.zeros_like(dqt)
    for load in loads:
        load.wait()
    lse_buf[0] = lse_buf[0] * LOG2E

    def arrive(j, *forward):
        kv_copy[j].wait_recv()
        for later in forward:
            kv_copy[later].start()

    def send(j, before=None):
        if before is None:
            stage[j] = acc[j].astype(BF16)
        else:
            g_copy[before].wait_recv()
            stage[j] = (acc[j] + came_in[before].astype(F32)).astype(BF16)
        g_copy[j].start()

    def step(v, carry):
        @pl.when(v == core + greet)
        def _():
            pl.semaphore_wait(barrier, len(partners))
            kv_copy[1].start()
            kv_copy[6].start()
            for copy in exchange:
                copy.start()

        @pl.when(v == core + 1)
        def _():
            for copy in exchange:
                copy.wait_recv()
            lse_buf[1] = lse_buf[1] * LOG2E

        @pl.when(v == 2)
        def _():
            arrive(1, 2)

        @pl.when(v == 4)
        def _():
            arrive(2, 3)
            arrive(6, 5)

        @pl.when(v == 6)
        def _():
            arrive(3, 4)

        @pl.when(v == 8)
        def _():
            send(3)
            arrive(4)

        @pl.when(v == 10)
        def _():
            send(4)
            send(2, 3)
            arrive(5)

        @pl.when(v == 11 + 2 * core)
        def _():
            dq_copy.start()

        @pl.when(v == 12)
        def _():
            send(5, 4)
            send(1, 2)

        j = lax.div(v, 2)
        even = lax.rem(v, 2) == 0
        other = jnp.where(core == 0, (v == 1) | (even & (v > 1) & (v < 12)), even)
        rows = jnp.where(other, 1, 0)
        ahead = TOK * (2 * j + rows * (1 - 2 * core))

        k = kv[j, 0]
        v = kv[j, 1]
        kt = k.T
        local = lax.broadcasted_iota(jnp.int32, (1, TOK), 1)
        high = local + ahead
        low = high - off_buf[rows]
        key_pos = lax.broadcasted_iota(jnp.int32, (TOK, TOK), 0)
        allowed = (key_pos >= low) & (key_pos <= high)
        dk = dv = None
        for h in range(HEADS):
            cols = slice(h * DH, (h + 1) * DH)
            q = q_buf[rows, :, cols]
            do = do_buf[rows, :, cols]
            score = dot_nt(k, q)
            prob = jnp.exp2(score * (SCALE * LOG2E) - lse_buf[rows, h : h + 1, :])
            prob = jnp.where(allowed, prob, 0.0)
            dprob = dot_nt(v, do)
            dscore = (prob * (dprob - del_buf[rows, h : h + 1, :])).astype(BF16)
            dv_h = dot_nn(prob.astype(BF16), do)
            dk_h = dot_nn(dscore, q)
            dv = dv_h if dv is None else dv + dv_h
            dk = dk_h if dk is None else dk + dk_h
            dqt[rows, h] += dot_nn(kt, dscore)
        acc[j, 0] += dk
        acc[j, 1] += dv
        return carry

    lax.fori_loop(core, UNITS + core, step, 0)
    send(6, 5)

    dq_copy.wait_recv()
    for h in range(HEADS):
        dq_st[:, h * DH : (h + 1) * DH] = (((dqt[0, h] + dq_in[h]) * SCALE).T).astype(BF16)
    outs = [pltpu.make_async_copy(dq_st, dq_out, out_sem.at[0])]
    outs[0].start()
    for j in (1, 6):
        g_copy[j].wait_recv()
    for n, (dst, scale) in enumerate(((dk_out, SCALE), (dv_out, 1.0))):
        summed = acc[0, n] + came_in[1, n].astype(F32) + came_in[6, n].astype(F32)
        dkv_st[n] = (summed * scale).astype(BF16)
        copy = pltpu.make_async_copy(dkv_st.at[n], dst, out_sem.at[1 + n])
        copy.start()
        outs.append(copy)
    for copy in exchange:
        copy.wait_send()
    for j in range(1, 7):
        kv_copy[j].wait_send()
        g_copy[j].wait_send()
    dq_copy.wait_send()
    for copy in outs:
        copy.wait()


def on_device(queries, out_grad, logsumexp, row_delta, doc_offset, key_states, value_states):
    kv_block = (2, TOK, DH)
    rows = (TOK, HEADS * DH)
    dma = pltpu.SemaphoreType.DMA
    return pl.pallas_call(
        kernel,
        out_shape=(
            jax.ShapeDtypeStruct(rows, BF16),
            jax.ShapeDtypeStruct((TOK, DH), BF16),
            jax.ShapeDtypeStruct((TOK, DH), BF16),
        ),
        in_specs=[pl.BlockSpec(memory_space=pl.ANY)] * 7,
        out_specs=[pl.BlockSpec(memory_space=pl.ANY)] * 3,
        scratch_shapes=[
            pltpu.VMEM((2, *rows), BF16),
            pltpu.VMEM((2, *rows), BF16),
            pltpu.VMEM((2, HEADS, TOK), F32),
            pltpu.VMEM((2, HEADS, TOK), F32),
            pltpu.VMEM((2, 1, TOK), jnp.int32),
            pltpu.VMEM((7, *kv_block), BF16),
            pltpu.VMEM((7, *kv_block), F32),
            pltpu.VMEM((2, HEADS, DH, TOK), F32),
            pltpu.VMEM((HEADS, DH, TOK), F32),
            pltpu.VMEM((7, *kv_block), BF16),
            pltpu.VMEM((7, *kv_block), BF16),
            pltpu.VMEM(rows, BF16),
            pltpu.VMEM(kv_block, BF16),
            dma((7,)), dma((5,)), dma((5,)), dma((7,)), dma((7,)), dma((7,)), dma((7,)), dma((2,)), dma((3,)),
        ],
        compiler_params=pltpu.CompilerParams(
            collective_id=0, has_side_effects=True, vmem_limit_bytes=60 << 20
        ),
        cost_estimate=pl.CostEstimate(flops=9_000_000_000, bytes_accessed=6_000_000, transcendentals=6_800_000),
        name="packed_attention_backward",
    )(queries, out_grad, logsumexp, row_delta, doc_offset.reshape(1, TOK), key_states, value_states)


def solution(mesh):
    both = ("outer", "inner")
    return jax.shard_map(
        on_device,
        mesh=mesh,
        in_specs=(P(both, None), P(both, None), P(None, both), P(None, both), P(both), P(both, None), P(both, None)),
        out_specs=(P(both, None), P(both, None), P(both, None)),
        check_vma=False,
    )
```

```python
import math

import jax
import jax.numpy as jnp
from jax import lax
from jax.experimental import pallas as pl
from jax.experimental.pallas import tpu as pltpu
from jax.sharding import PartitionSpec as P

MESH = pl.DeviceIdType.MESH
F32 = jnp.float32
BF16 = jnp.bfloat16
HEADS = 8
DH = 128
TOK = 256
SCALE = 1.0 / math.sqrt(DH)
LOG2E = math.log2(math.e)


def dot_nt(a, b):
    return lax.dot_general(a, b, (((1,), (1,)), ((), ())), preferred_element_type=F32)


def dot_nn(a, b):
    return jnp.dot(a, b, preferred_element_type=F32)


def kernel(
    q_hbm, do_hbm, lse_hbm, del_hbm, off_hbm, k_hbm, v_hbm,
    dq_out, dk_out, dv_out,
    q_buf, do_buf, lse_buf, del_buf, off_buf, kv, acc, dqt, dq_in, stage, came_in,
    dq_st, dkv_st,
    load_sem, ex_send, ex_recv, kv_send, kv_recv, g_send, g_recv, dq_sem, out_sem,
):
    outer, inner = lax.axis_size("outer"), lax.axis_size("inner")
    total = outer * inner
    me = lax.axis_index("outer") * inner + lax.axis_index("inner")
    core = lax.rem(me, 2)
    greet = 0

    def at(chips):
        there = lax.rem(me + 2 * chips + total, total)
        return (lax.div(there, inner), lax.rem(there, inner))

    sib_index = me + 1 - 2 * core
    sibling = (lax.div(sib_index, inner), lax.rem(sib_index, inner))

    loads = [
        pltpu.make_async_copy(src, dst, load_sem.at[n])
        for n, (src, dst) in enumerate((
            (k_hbm, kv.at[0, 0]), (v_hbm, kv.at[0, 1]),
            (q_hbm, q_buf.at[0]), (do_hbm, do_buf.at[0]),
            (lse_hbm, lse_buf.at[0]), (del_hbm, del_buf.at[0]), (off_hbm, off_buf.at[0]),
        ))
    ]
    for load in loads:
        load.start()

    barrier = pltpu.get_barrier_semaphore()
    partners = [sibling] + [at(chips) for chips in (1, -1, -6)]
    for partner in partners:
        pl.semaphore_signal(barrier, inc=1, device_id=partner, device_id_type=MESH)

    def remote(src, dst, send, recv, where):
        return pltpu.make_async_remote_copy(
            src_ref=src, dst_ref=dst, send_sem=send, recv_sem=recv, device_id=where, device_id_type=MESH
        )

    exchange = [
        remote(src, dst, ex_send.at[n], ex_recv.at[n], sibling)
        for n, (src, dst) in enumerate((
            (q_hbm, q_buf.at[1]), (do_hbm, do_buf.at[1]),
            (lse_hbm, lse_buf.at[1]), (del_hbm, del_buf.at[1]), (off_hbm, off_buf.at[1]),
        ))
    ]
    kv_from = {1: (0, 1), 2: (1, 1), 3: (2, 1), 6: (0, 6), 5: (6, -1), 4: (5, -1)}
    kv_copy = {
        j: remote(kv.at[src], kv.at[j], kv_send.at[j], kv_recv.at[j], at(chips))
        for j, (src, chips) in kv_from.items()
    }
    g_to = {1: -1, 2: -1, 3: -1, 4: -1, 5: -1, 6: -1}
    g_copy = {
        j: remote(stage.at[j], came_in.at[j], g_send.at[j], g_recv.at[j], at(chips)) for j, chips in g_to.items()
    }
    dq_copy = remote(dqt.at[1], dq_in, dq_sem.at[0], dq_sem.at[1], sibling)

    acc[...] = jnp.zeros_like(acc)
    dqt[...] = jnp.zeros_like(dqt)
    for load in loads:
        load.wait()
    lse_buf[0] = lse_buf[0] * LOG2E

    def arrive(j, *forward):
        kv_copy[j].wait_recv()
        for later in forward:
            kv_copy[later].start()

    def send(j, before=None):
        if before is None:
            stage[j] = acc[j].astype(BF16)
        else:
            g_copy[before].wait_recv()
            stage[j] = (acc[j] + came_in[before].astype(F32)).astype(BF16)
        g_copy[j].start()

    def tiles(j, row_blocks):
        k = kv[j, 0]
        v = kv[j, 1]
        kt = k.T
        local = lax.broadcasted_iota(jnp.int32, (1, TOK), 1)
        key_pos = lax.broadcasted_iota(jnp.int32, (TOK, TOK), 0)
        dk = dv = None
        for rows in row_blocks:
            high = local + TOK * (2 * j + rows * (1 - 2 * core))
            low = high - off_buf[rows]
            allowed = (key_pos >= low) & (key_pos <= high)
            for h in range(HEADS):
                cols = slice(h * DH, (h + 1) * DH)
                q = q_buf[rows, :, cols]
                do = do_buf[rows, :, cols]
                score = dot_nt(k, q)
                prob = jnp.exp2(score * (SCALE * LOG2E) - lse_buf[rows, h : h + 1, :])
                prob = jnp.where(allowed, prob, 0.0)
                dprob = dot_nt(v, do)
                dscore = (prob * (dprob - del_buf[rows, h : h + 1, :])).astype(BF16)
                dv_h = dot_nn(prob.astype(BF16), do)
                dk_h = dot_nn(dscore, q)
                dv = dv_h if dv is None else dv + dv_h
                dk = dk_h if dk is None else dk + dk_h
                dqt[rows, h] += dot_nn(kt, dscore)
        acc[j, 0] += dk
        acc[j, 1] += dv

    def single(u, carry):
        @pl.when(u == greet)
        def _():
            pl.semaphore_wait(barrier, len(partners))
            kv_copy[1].start()
            kv_copy[6].start()
            for copy in exchange:
                copy.start()

        @pl.when(u == 1)
        def _():
            for copy in exchange:
                copy.wait_recv()
            lse_buf[1] = lse_buf[1] * LOG2E

        @pl.when(u == 2 - core)
        def _():
            arrive(6, 5)

        @pl.when(u == 2)
        def _():
            arrive(1, 2)

        tiles(6 * lax.div(u + core, 2), (lax.rem(u, 2),))
        return carry

    def double(t, carry):
        @pl.when(t == 0)
        def _():
            arrive(5, 4)
            send(6)
            arrive(2, 3)

        @pl.when(t == 1)
        def _():
            arrive(4)
            send(5, 6)

        @pl.when(t == 2)
        def _():
            arrive(3)
            send(4, 5)

        @pl.when(t == 3)
        def _():
            send(3, 4)

        @pl.when(t == 4)
        def _():
            send(2, 3)

        tiles(5 - t, (1, 0))
        return carry

    lax.fori_loop(0, 3, single, 0)
    lax.fori_loop(0, 5, double, 0)
    dq_copy.start()
    send(1, 2)

    dq_copy.wait_recv()
    for h in range(HEADS):
        dq_st[:, h * DH : (h + 1) * DH] = (((dqt[0, h] + dq_in[h]) * SCALE).T).astype(BF16)
    outs = [pltpu.make_async_copy(dq_st, dq_out, out_sem.at[0])]
    outs[0].start()
    for j in (1,):
        g_copy[j].wait_recv()
    for n, (dst, scale) in enumerate(((dk_out, SCALE), (dv_out, 1.0))):
        summed = acc[0, n]
        for j in (1,):
            summed = summed + came_in[j, n].astype(F32)
        dkv_st[n] = (summed * scale).astype(BF16)
        copy = pltpu.make_async_copy(dkv_st.at[n], dst, out_sem.at[1 + n])
        copy.start()
        outs.append(copy)
    for copy in exchange:
        copy.wait_send()
    for j in range(1, 7):
        kv_copy[j].wait_send()
        g_copy[j].wait_send()
    dq_copy.wait_send()
    for copy in outs:
        copy.wait()


def place(dq_in, dk_in, dv_in, dq_out, dk_out, dv_out):
    dq_out[...] = dq_in[...]
    dk_out[...] = dk_in[...]
    dv_out[...] = dv_in[...]


def on_device(queries, out_grad, logsumexp, row_delta, doc_offset, key_states, value_states):
    kv_block = (2, TOK, DH)
    rows = (TOK, HEADS * DH)
    dma = pltpu.SemaphoreType.DMA
    shapes = (
        jax.ShapeDtypeStruct(rows, BF16),
        jax.ShapeDtypeStruct((TOK, DH), BF16),
        jax.ShapeDtypeStruct((TOK, DH), BF16),
    )
    grads = pl.pallas_call(
        kernel,
        out_shape=shapes,
        in_specs=[pl.BlockSpec(memory_space=pl.ANY)] * 7,
        out_specs=[pl.BlockSpec(memory_space=pl.ANY)] * 3,
        scratch_shapes=[
            pltpu.VMEM((2, *rows), BF16),
            pltpu.VMEM((2, *rows), BF16),
            pltpu.VMEM((2, HEADS, TOK), F32),
            pltpu.VMEM((2, HEADS, TOK), F32),
            pltpu.VMEM((2, 1, TOK), jnp.int32),
            pltpu.VMEM((7, *kv_block), BF16),
            pltpu.VMEM((7, *kv_block), F32),
            pltpu.VMEM((2, HEADS, DH, TOK), F32),
            pltpu.VMEM((HEADS, DH, TOK), F32),
            pltpu.VMEM((7, *kv_block), BF16),
            pltpu.VMEM((7, *kv_block), BF16),
            pltpu.VMEM(rows, BF16),
            pltpu.VMEM(kv_block, BF16),
            dma((7,)), dma((5,)), dma((5,)), dma((7,)), dma((7,)), dma((7,)), dma((7,)), dma((2,)), dma((3,)),
        ],
        compiler_params=pltpu.CompilerParams(
            collective_id=0, has_side_effects=True, vmem_limit_bytes=60 << 20
        ),
        cost_estimate=pl.CostEstimate(flops=9_000_000_000, bytes_accessed=6_000_000, transcendentals=6_800_000),
        name="packed_attention_backward",
    )(queries, out_grad, logsumexp, row_delta, doc_offset.reshape(1, TOK), key_states, value_states)
    return pl.pallas_call(place, out_shape=shapes, name="place")(*grads)


def solution(mesh):
    both = ("outer", "inner")
    return jax.shard_map(
        on_device,
        mesh=mesh,
        in_specs=(P(both, None), P(both, None), P(None, both), P(None, both), P(both), P(both, None), P(both, None)),
        out_specs=(P(both, None), P(both, None), P(both, None)),
        check_vma=False,
    )
```

```python
import math

import jax
import jax.numpy as jnp
from jax import lax
from jax.experimental import pallas as pl
from jax.experimental.pallas import tpu as pltpu
from jax.sharding import PartitionSpec as P

MESH = pl.DeviceIdType.MESH
F32 = jnp.float32
BF16 = jnp.bfloat16
HEADS = 8
DH = 128
TOK = 256
SCALE = 1.0 / math.sqrt(DH)
LOG2E = math.log2(math.e)


def dot_nt(a, b):
    return lax.dot_general(a, b, (((1,), (1,)), ((), ())), preferred_element_type=F32)


def dot_nn(a, b):
    return jnp.dot(a, b, preferred_element_type=F32)


def kernel(
    q_hbm, do_hbm, lse_hbm, del_hbm, off_hbm, k_hbm, v_hbm,
    dq_out, dk_out, dv_out,
    q_buf, do_buf, lse_buf, del_buf, off_buf, kv, acc, dqt, dq_in, stage, came_in,
    dq_st, dkv_st, spare,
    load_sem, ex_send, ex_recv, kv_send, kv_recv, g_send, g_recv, dq_sem, out_sem,
    help_send, help_recv,
):
    outer, inner = lax.axis_size("outer"), lax.axis_size("inner")
    total = outer * inner
    me = lax.axis_index("outer") * inner + lax.axis_index("inner")
    core = lax.rem(me, 2)
    greet = 0

    def at(chips):
        there = lax.rem(me + 2 * chips + total, total)
        return (lax.div(there, inner), lax.rem(there, inner))

    sib_index = me + 1 - 2 * core
    sibling = (lax.div(sib_index, inner), lax.rem(sib_index, inner))

    loads = [
        pltpu.make_async_copy(src, dst, load_sem.at[n])
        for n, (src, dst) in enumerate((
            (k_hbm, kv.at[0, 0]), (v_hbm, kv.at[0, 1]),
            (q_hbm, q_buf.at[0]), (do_hbm, do_buf.at[0]),
            (lse_hbm, lse_buf.at[0]), (del_hbm, del_buf.at[0]), (off_hbm, off_buf.at[0]),
        ))
    ]
    for load in loads:
        load.start()

    barrier = pltpu.get_barrier_semaphore()
    chip, last = lax.div(me, 2), total // 2 - 1
    before = chip >= 1
    after = chip < last
    sixth = chip + 6 <= last
    short = (chip == last - 5) | (chip == last - 4)
    helper = (chip == last - 7) | (chip == last - 6)
    pl.semaphore_signal(barrier, inc=1, device_id=sibling, device_id_type=MESH)
    told = ((after, 1), (before, -1), (chip >= 6, -6), (helper, 2), (chip == last, -7))
    for there, chips in told:
        @pl.when(there)
        def _():
            pl.semaphore_signal(barrier, inc=1, device_id=at(chips), device_id_type=MESH)

    def remote(src, dst, send, recv, where):
        return pltpu.make_async_remote_copy(
            src_ref=src, dst_ref=dst, send_sem=send, recv_sem=recv, device_id=where, device_id_type=MESH
        )

    exchange = [
        remote(src, dst, ex_send.at[n], ex_recv.at[n], sibling)
        for n, (src, dst) in enumerate((
            (q_hbm, q_buf.at[1]), (do_hbm, do_buf.at[1]),
            (lse_hbm, lse_buf.at[1]), (del_hbm, del_buf.at[1]), (off_hbm, off_buf.at[1]),
        ))
    ]
    kv_from = {1: (0, 1), 2: (1, 1), 3: (2, 1), 6: (0, 6), 5: (6, -1), 4: (5, -1)}
    kv_copy = {
        j: remote(kv.at[src], kv.at[j], kv_send.at[j], kv_recv.at[j], at(chips))
        for j, (src, chips) in kv_from.items()
    }
    help_copy = [
        remote(kv.at[0], spare.at[0], help_send.at[0], help_recv.at[0], at(-2)),
        remote(spare.at[0], kv.at[5], help_send.at[1], kv_recv.at[5], at(7)),
        remote(spare.at[0], spare.at[1], help_send.at[2], help_recv.at[1], at(-1)),
        remote(spare.at[1], kv.at[4], help_send.at[3], kv_recv.at[4], at(7)),
    ]
    g_to = {1: -1, 2: -1, 3: -1, 4: -1, 5: -1, 6: -1}
    g_copy = {
        j: remote(stage.at[j], came_in.at[j], g_send.at[j], g_recv.at[j], at(chips)) for j, chips in g_to.items()
    }
    dq_copy = remote(dqt.at[1], dq_in, dq_sem.at[0], dq_sem.at[1], sibling)

    acc[...] = jnp.zeros_like(acc)
    dqt[...] = jnp.zeros_like(dqt)
    for load in loads:
        load.wait()
    lse_buf[0] = lse_buf[0] * LOG2E

    def passes(j):
        return {1: after, 6: sixth, 2: before & after, 3: (chip >= 2) & after, 5: chip >= 6, 4: chip >= 5}[j]

    def arrive(j, forward=None):
        pl.when(chip >= j)(kv_copy[j].wait_recv)
        if forward is not None:
            pl.when(passes(forward))(kv_copy[forward].start)

    def send(j, chained=None):
        @pl.when(chip >= j)
        def _():
            stage[j] = acc[j].astype(BF16)
            if chained is not None:
                @pl.when(after)
                def _():
                    g_copy[chained].wait_recv()
                    stage[j] = (acc[j] + came_in[chained].astype(F32)).astype(BF16)
            g_copy[j].start()

    def tiles(j, row_blocks):
        k = kv[j, 0]
        v = kv[j, 1]
        kt = k.T
        local = lax.broadcasted_iota(jnp.int32, (1, TOK), 1)
        key_pos = lax.broadcasted_iota(jnp.int32, (TOK, TOK), 0)
        dk = dv = None
        for rows in row_blocks:
            high = local + TOK * (2 * j + rows * (1 - 2 * core))
            low = high - off_buf[rows]
            allowed = (key_pos >= low) & (key_pos <= high)
            for h in range(HEADS):
                cols = slice(h * DH, (h + 1) * DH)
                q = q_buf[rows, :, cols]
                do = do_buf[rows, :, cols]
                score = dot_nt(k, q)
                prob = jnp.exp2(score * (SCALE * LOG2E) - lse_buf[rows, h : h + 1, :])
                prob = jnp.where(allowed, prob, 0.0)
                dprob = dot_nt(v, do)
                dscore = (prob * (dprob - del_buf[rows, h : h + 1, :])).astype(BF16)
                dv_h = dot_nn(prob.astype(BF16), do)
                dk_h = dot_nn(dscore, q)
                dv = dv_h if dv is None else dv + dv_h
                dk = dk_h if dk is None else dk + dk_h
                dqt[rows, h] += dot_nn(kt, dscore)
        acc[j, 0] += dk
        acc[j, 1] += dv

    def single(u, carry):
        @pl.when(u == greet)
        def _():
            ready = [jnp.where(there, 1, 0) for there in (after, before, sixth, short, chip == last - 7)]
            pl.semaphore_wait(barrier, 1 + sum(ready))
            pl.when(sixth)(kv_copy[6].start)
            pl.when(after)(kv_copy[1].start)
            pl.when(short)(help_copy[0].start)
            for copy in exchange:
                copy.start()

        @pl.when(u == 1)
        def _():
            for copy in exchange:
                copy.wait_recv()
            lse_buf[1] = lse_buf[1] * LOG2E

        @pl.when(u == 2 - core)
        def _():
            arrive(6, 5)
            pl.when(helper)(help_copy[0].wait_recv)
            pl.when(chip == last - 7)(help_copy[1].start)
            pl.when(chip == last - 6)(help_copy[2].start)

        @pl.when(u == 2)
        def _():
            arrive(1, 2)

        j = 6 * lax.div(u + core, 2)
        pl.when(chip >= j)(lambda: tiles(j, (lax.rem(u, 2),)))
        return carry

    def double(t, carry):
        @pl.when(t == 0)
        def _():
            arrive(5, 4)
            send(6)
            arrive(2, 3)

            @pl.when(chip == last - 7)
            def _():
                help_copy[2].wait_recv()
                help_copy[3].start()

        @pl.when(t == 1)
        def _():
            arrive(4)
            send(5, 6)

        @pl.when(t == 2)
        def _():
            arrive(3)
            send(4, 5)

        @pl.when(t == 3)
        def _():
            send(3, 4)

        @pl.when(t == 4)
        def _():
            send(2, 3)

        pl.when(chip >= 5 - t)(lambda: tiles(5 - t, (1, 0)))
        return carry

    lax.fori_loop(0, 3, single, 0)
    lax.fori_loop(0, 5, double, 0)
    dq_copy.start()
    send(1, 2)

    dq_copy.wait_recv()
    for h in range(HEADS):
        dq_st[:, h * DH : (h + 1) * DH] = (((dqt[0, h] + dq_in[h]) * SCALE).T).astype(BF16)
    outs = [pltpu.make_async_copy(dq_st, dq_out, out_sem.at[0])]
    outs[0].start()

    @pl.when(after)
    def _():
        g_copy[1].wait_recv()
        acc[0] = acc[0] + came_in[1].astype(F32)

    for n, (dst, scale) in enumerate(((dk_out, SCALE), (dv_out, 1.0))):
        dkv_st[n] = (acc[0, n] * scale).astype(BF16)
        copy = pltpu.make_async_copy(dkv_st.at[n], dst, out_sem.at[1 + n])
        copy.start()
        outs.append(copy)
    for copy in exchange:
        copy.wait_send()
    for j in range(1, 7):
        pl.when(passes(j))(kv_copy[j].wait_send)
        pl.when(chip >= j)(g_copy[j].wait_send)
    pl.when(short)(help_copy[0].wait_send)
    pl.when(chip == last - 7)(help_copy[1].wait_send)
    pl.when(chip == last - 6)(help_copy[2].wait_send)
    pl.when(chip == last - 7)(help_copy[3].wait_send)
    dq_copy.wait_send()
    for copy in outs:
        copy.wait()


def place(dq_in, dk_in, dv_in, dq_out, dk_out, dv_out):
    dq_out[...] = dq_in[...]
    dk_out[...] = dk_in[...]
    dv_out[...] = dv_in[...]


def on_device(queries, out_grad, logsumexp, row_delta, doc_offset, key_states, value_states):
    kv_block = (2, TOK, DH)
    rows = (TOK, HEADS * DH)
    dma = pltpu.SemaphoreType.DMA
    shapes = (
        jax.ShapeDtypeStruct(rows, BF16),
        jax.ShapeDtypeStruct((TOK, DH), BF16),
        jax.ShapeDtypeStruct((TOK, DH), BF16),
    )
    grads = pl.pallas_call(
        kernel,
        out_shape=shapes,
        in_specs=[pl.BlockSpec(memory_space=pl.ANY)] * 7,
        out_specs=[pl.BlockSpec(memory_space=pl.ANY)] * 3,
        scratch_shapes=[
            pltpu.VMEM((2, *rows), BF16),
            pltpu.VMEM((2, *rows), BF16),
            pltpu.VMEM((2, HEADS, TOK), F32),
            pltpu.VMEM((2, HEADS, TOK), F32),
            pltpu.VMEM((2, 1, TOK), jnp.int32),
            pltpu.VMEM((7, *kv_block), BF16),
            pltpu.VMEM((7, *kv_block), F32),
            pltpu.VMEM((2, HEADS, DH, TOK), F32),
            pltpu.VMEM((HEADS, DH, TOK), F32),
            pltpu.VMEM((7, *kv_block), BF16),
            pltpu.VMEM((7, *kv_block), BF16),
            pltpu.VMEM(rows, BF16),
            pltpu.VMEM(kv_block, BF16),
            pltpu.VMEM((2, *kv_block), BF16),
            dma((7,)), dma((5,)), dma((5,)), dma((7,)), dma((7,)), dma((7,)), dma((7,)), dma((2,)), dma((3,)),
            dma((4,)), dma((2,)),
        ],
        compiler_params=pltpu.CompilerParams(
            collective_id=0, has_side_effects=True, vmem_limit_bytes=60 << 20
        ),
        cost_estimate=pl.CostEstimate(flops=9_000_000_000, bytes_accessed=6_000_000, transcendentals=6_800_000),
        name="packed_attention_backward",
    )(queries, out_grad, logsumexp, row_delta, doc_offset.reshape(1, TOK), key_states, value_states)
    return pl.pallas_call(place, out_shape=shapes, name="place")(*grads)


def solution(mesh):
    both = ("outer", "inner")
    return jax.shard_map(
        on_device,
        mesh=mesh,
        in_specs=(P(both, None), P(both, None), P(None, both), P(None, both), P(both), P(both, None), P(both, None)),
        out_specs=(P(both, None), P(both, None), P(both, None)),
        check_vma=False,
    )
```

```python
import math

import jax
import jax.numpy as jnp
from jax import lax
from jax.experimental import pallas as pl
from jax.experimental.pallas import tpu as pltpu
from jax.sharding import PartitionSpec as P

MESH = pl.DeviceIdType.MESH
F32 = jnp.float32
BF16 = jnp.bfloat16
HEADS = 8
DH = 128
TOK = 256
SCALE = 1.0 / math.sqrt(DH)
LOG2E = math.log2(math.e)


def dot_nt(a, b):
    return lax.dot_general(a, b, (((1,), (1,)), ((), ())), preferred_element_type=F32)


def dot_nn(a, b):
    return jnp.dot(a, b, preferred_element_type=F32)


class Both:
    def __init__(self, copies):
        self.copies = copies

    def start(self):
        for copy in self.copies:
            copy.start()

    def wait_recv(self):
        for copy in self.copies:
            copy.wait_recv()

    def wait_send(self):
        for copy in self.copies:
            copy.wait_send()


def kernel(
    q_hbm, do_hbm, lse_hbm, del_hbm, off_hbm, k_hbm, v_hbm,
    dq_out, dk_out, dv_out,
    q_buf, do_buf, lse_buf, del_buf, off_buf, kv, acc, dqt, dq_in, stage, came_in,
    dq_st, dkv_st, spare,
    load_sem, ex_send, ex_recv, kv_send, kv_recv, g_send, g_recv, dq_sem, out_sem,
    help_send, help_recv,
):
    outer, inner = lax.axis_size("outer"), lax.axis_size("inner")
    total = outer * inner
    me = lax.axis_index("outer") * inner + lax.axis_index("inner")
    core = lax.rem(me, 2)
    greet = 0

    def at(chips):
        there = lax.rem(me + 2 * chips + total, total)
        return (lax.div(there, inner), lax.rem(there, inner))

    sib_index = me + 1 - 2 * core
    sibling = (lax.div(sib_index, inner), lax.rem(sib_index, inner))

    loads = [
        pltpu.make_async_copy(src, dst, load_sem.at[n])
        for n, (src, dst) in enumerate((
            (k_hbm, kv.at[0, 0]), (v_hbm, kv.at[0, 1]),
            (q_hbm, q_buf.at[0]), (do_hbm, do_buf.at[0]),
            (lse_hbm, lse_buf.at[0]), (del_hbm, del_buf.at[0]), (off_hbm, off_buf.at[0]),
        ))
    ]
    for load in loads:
        load.start()

    barrier = pltpu.get_barrier_semaphore()
    chip, last = lax.div(me, 2), total // 2 - 1
    before = chip >= 1
    after = chip < last
    sixth = chip + 6 <= last
    short = (chip == last - 5) | (chip == last - 4)
    helper = (chip == last - 7) | (chip == last - 6)
    pl.semaphore_signal(barrier, inc=1, device_id=sibling, device_id_type=MESH)
    told = ((after, 1), (before, -1), (chip >= 6, -6), (helper, 2), (chip == last, -7))
    for there, chips in told:
        @pl.when(there)
        def _():
            pl.semaphore_signal(barrier, inc=1, device_id=at(chips), device_id_type=MESH)

    def remote(src, dst, send, recv, where):
        return pltpu.make_async_remote_copy(
            src_ref=src, dst_ref=dst, send_sem=send, recv_sem=recv, device_id=where, device_id_type=MESH
        )

    def halves(src, dst, send, recv, where):
        return Both([remote(src.at[n], dst.at[n], send.at[n], recv.at[n], where) for n in range(2)])

    exchange = [
        remote(src, dst, ex_send.at[n], ex_recv.at[n], sibling)
        for n, (src, dst) in enumerate((
            (q_hbm, q_buf.at[1]), (do_hbm, do_buf.at[1]),
            (lse_hbm, lse_buf.at[1]), (del_hbm, del_buf.at[1]), (off_hbm, off_buf.at[1]),
        ))
    ]
    kv_from = {1: (0, 1), 2: (1, 1), 3: (2, 1), 6: (0, 6), 5: (6, -1), 4: (5, -1)}
    kv_copy = {
        j: halves(kv.at[src], kv.at[j], kv_send.at[j], kv_recv.at[j], at(chips))
        for j, (src, chips) in kv_from.items()
    }
    help_copy = [
        halves(kv.at[0], spare.at[0], help_send.at[0], help_recv.at[0], at(-2)),
        halves(spare.at[0], kv.at[5], help_send.at[1], kv_recv.at[5], at(7)),
        halves(spare.at[0], spare.at[1], help_send.at[2], help_recv.at[1], at(-1)),
        halves(spare.at[1], kv.at[4], help_send.at[3], kv_recv.at[4], at(7)),
    ]
    g_to = {1: -1, 2: -1, 3: -1, 4: -1, 5: -1, 6: -1}
    g_copy = {
        j: halves(stage.at[j], came_in.at[j], g_send.at[j], g_recv.at[j], at(chips)) for j, chips in g_to.items()
    }
    dq_copy = remote(dqt.at[1], dq_in, dq_sem.at[0], dq_sem.at[1], sibling)

    acc[...] = jnp.zeros_like(acc)
    dqt[...] = jnp.zeros_like(dqt)
    for load in loads:
        load.wait()
    lse_buf[0] = lse_buf[0] * LOG2E

    def passes(j):
        return {1: after, 6: sixth, 2: before & after, 3: (chip >= 2) & after, 5: chip >= 6, 4: chip >= 5}[j]

    def arrive(j, forward=None):
        for n in range(2):
            pl.when(chip >= j)(kv_copy[j].copies[n].wait_recv)
            if forward is not None:
                pl.when(passes(forward))(kv_copy[forward].copies[n].start)

    def send(j, chained=None):
        @pl.when(chip >= j)
        def _():
            for n in range(2):
                if chained is not None:
                    @pl.when(after)
                    def _():
                        g_copy[chained].copies[n].wait_recv()
                        acc[j, n] = acc[j, n] + came_in[chained, n].astype(F32)

                stage[j, n] = acc[j, n].astype(BF16)
                g_copy[j].copies[n].start()

    def tiles(j, row_blocks):
        k = kv[j, 0]
        v = kv[j, 1]
        kt = k.T
        local = lax.broadcasted_iota(jnp.int32, (1, TOK), 1)
        key_pos = lax.broadcasted_iota(jnp.int32, (TOK, TOK), 0)
        dk = dv = None
        for rows in row_blocks:
            high = local + TOK * (2 * j + rows * (1 - 2 * core))
            low = high - off_buf[rows]
            allowed = (key_pos >= low) & (key_pos <= high)
            for h in range(HEADS):
                cols = slice(h * DH, (h + 1) * DH)
                q = q_buf[rows, :, cols]
                do = do_buf[rows, :, cols]
                score = dot_nt(k, q)
                prob = jnp.exp2(score * (SCALE * LOG2E) - lse_buf[rows, h : h + 1, :])
                prob = jnp.where(allowed, prob, 0.0)
                dprob = dot_nt(v, do)
                dscore = (prob * (dprob - del_buf[rows, h : h + 1, :])).astype(BF16)
                dv_h = dot_nn(prob.astype(BF16), do)
                dk_h = dot_nn(dscore, q)
                dv = dv_h if dv is None else dv + dv_h
                dk = dk_h if dk is None else dk + dk_h
                dqt[rows, h] += dot_nn(kt, dscore)
        acc[j, 0] += dk
        acc[j, 1] += dv

    def single(u, carry):
        @pl.when(u == greet)
        def _():
            ready = [jnp.where(there, 1, 0) for there in (after, before, sixth, short, chip == last - 7)]
            pl.semaphore_wait(barrier, 1 + sum(ready))
            pl.when(sixth)(kv_copy[6].start)
            pl.when(after)(kv_copy[1].start)
            pl.when(short)(help_copy[0].start)
            for copy in exchange:
                copy.start()

        @pl.when(u == 1)
        def _():
            for copy in exchange:
                copy.wait_recv()
            lse_buf[1] = lse_buf[1] * LOG2E

        @pl.when(u == 2 - core)
        def _():
            arrive(6, 5)
            pl.when(helper)(help_copy[0].wait_recv)
            pl.when(chip == last - 7)(help_copy[1].start)
            pl.when(chip == last - 6)(help_copy[2].start)

        @pl.when(u == 2)
        def _():
            arrive(1, 2)

        j = 6 * lax.div(u + core, 2)
        pl.when(chip >= j)(lambda: tiles(j, (lax.rem(u, 2),)))
        return carry

    def double(t, carry):
        @pl.when(t == 0)
        def _():
            arrive(5, 4)
            send(6)
            arrive(2, 3)

            @pl.when(chip == last - 7)
            def _():
                help_copy[2].wait_recv()
                help_copy[3].start()

        @pl.when(t == 1)
        def _():
            arrive(4)
            send(5, 6)

        @pl.when(t == 2)
        def _():
            arrive(3)
            send(4, 5)

        @pl.when(t == 3)
        def _():
            send(3, 4)

        @pl.when(t == 4)
        def _():
            send(2, 3)

        pl.when(chip >= 5 - t)(lambda: tiles(5 - t, (1, 0)))
        return carry

    lax.fori_loop(0, 3, single, 0)
    lax.fori_loop(0, 5, double, 0)
    dq_copy.start()
    send(1, 2)

    dq_copy.wait_recv()
    for h in range(HEADS):
        dq_st[:, h * DH : (h + 1) * DH] = (((dqt[0, h] + dq_in[h]) * SCALE).T).astype(BF16)
    outs = [pltpu.make_async_copy(dq_st, dq_out, out_sem.at[0])]
    outs[0].start()

    for n, (dst, scale) in enumerate(((dk_out, SCALE), (dv_out, 1.0))):
        @pl.when(after)
        def _():
            g_copy[1].copies[n].wait_recv()
            acc[0, n] = acc[0, n] + came_in[1, n].astype(F32)

        dkv_st[n] = (acc[0, n] * scale).astype(BF16)
        copy = pltpu.make_async_copy(dkv_st.at[n], dst, out_sem.at[1 + n])
        copy.start()
        outs.append(copy)
    for copy in exchange:
        copy.wait_send()
    for j in range(1, 7):
        pl.when(passes(j))(kv_copy[j].wait_send)
        pl.when(chip >= j)(g_copy[j].wait_send)
    pl.when(short)(help_copy[0].wait_send)
    pl.when(chip == last - 7)(help_copy[1].wait_send)
    pl.when(chip == last - 6)(help_copy[2].wait_send)
    pl.when(chip == last - 7)(help_copy[3].wait_send)
    dq_copy.wait_send()
    for copy in outs:
        copy.wait()


def place(dq_in, dk_in, dv_in, dq_out, dk_out, dv_out):
    dq_out[...] = dq_in[...]
    dk_out[...] = dk_in[...]
    dv_out[...] = dv_in[...]


def on_device(queries, out_grad, logsumexp, row_delta, doc_offset, key_states, value_states):
    kv_block = (2, TOK, DH)
    rows = (TOK, HEADS * DH)
    dma = pltpu.SemaphoreType.DMA
    shapes = (
        jax.ShapeDtypeStruct(rows, BF16),
        jax.ShapeDtypeStruct((TOK, DH), BF16),
        jax.ShapeDtypeStruct((TOK, DH), BF16),
    )
    grads = pl.pallas_call(
        kernel,
        out_shape=shapes,
        in_specs=[pl.BlockSpec(memory_space=pl.ANY)] * 7,
        out_specs=[pl.BlockSpec(memory_space=pl.ANY)] * 3,
        scratch_shapes=[
            pltpu.VMEM((2, *rows), BF16),
            pltpu.VMEM((2, *rows), BF16),
            pltpu.VMEM((2, HEADS, TOK), F32),
            pltpu.VMEM((2, HEADS, TOK), F32),
            pltpu.VMEM((2, 1, TOK), jnp.int32),
            pltpu.VMEM((7, *kv_block), BF16),
            pltpu.VMEM((7, *kv_block), F32),
            pltpu.VMEM((2, HEADS, DH, TOK), F32),
            pltpu.VMEM((HEADS, DH, TOK), F32),
            pltpu.VMEM((7, *kv_block), BF16),
            pltpu.VMEM((7, *kv_block), BF16),
            pltpu.VMEM(rows, BF16),
            pltpu.VMEM(kv_block, BF16),
            pltpu.VMEM((2, *kv_block), BF16),
            dma((7,)), dma((5,)), dma((5,)), dma((7, 2)), dma((7, 2)), dma((7, 2)), dma((7, 2)), dma((2,)), dma((3,)),
            dma((4, 2)), dma((2, 2)),
        ],
        compiler_params=pltpu.CompilerParams(
            collective_id=0, has_side_effects=True, vmem_limit_bytes=60 << 20
        ),
        cost_estimate=pl.CostEstimate(flops=9_000_000_000, bytes_accessed=6_000_000, transcendentals=6_800_000),
        name="packed_attention_backward",
    )(queries, out_grad, logsumexp, row_delta, doc_offset.reshape(1, TOK), key_states, value_states)
    return pl.pallas_call(place, out_shape=shapes, name="place")(*grads)


def solution(mesh):
    both = ("outer", "inner")
    return jax.shard_map(
        on_device,
        mesh=mesh,
        in_specs=(P(both, None), P(both, None), P(None, both), P(None, both), P(both), P(both, None), P(both, None)),
        out_specs=(P(both, None), P(both, None), P(both, None)),
        check_vma=False,
    )
```
